256 devices in a mesh: prow: 16 (over x, y), pcol: 16 (over z, core).
Axes of the slice: x: 4, y: 4, z: 8, core: 2. Of those that a mesh axis runs over, the one named last changes fastest.
Arguments:
- seeds: int32 [64, 400], P(None, 'pcol'), may hold values from 0 to 1073741823
- tile_owner: int32 [64], replicated, may hold values from 0 to 15, as said below
- vector: float32 [204800], P(('pcol', 'prow')), may hold values from -6 to 6
- rhs: float32 [32768], P('prow'), may hold values from -6 to 6
- panel: bfloat16 [32768, 4096], P('prow', 'pcol'), may hold values from -0.25 to 0.25
- tile_scales: float32 [64, 8], P('prow'), may hold values from 0.1 to 0.5
- inverses: bfloat16 [4096, 512], P('pcol'), as said below
Outputs:
- solved: float32 [4096], P('pcol')
- updated: float32 [32768], P(('prow', 'pcol'))
The draws below stay inside these ranges and needn't reach their ends.
Inputs may be any that keep to these rules, and one draw needn't show every extreme that they name: tile_owner[i] = (i + a) mod (16) for one a (so a = tile_owner[0]). Each block of 512 rows of inverses is unit lower triangular.
All inputs are finite; a program needn't handle non-finite values.
Results may differ from the reference program's by a relative error of at most 0.0003.
Values sent between devices are 32-bit elements; how exact they have to be, the bound alone decides.
No kernel may reach another device: no remote copies, remote signals or barrier semaphores. Data moves between devices by JAX's collectives and lax.ppermute only.
A program may use at most 64 MiB of HBM per device.

```python
import math
import jax
import jax.numpy as jnp
from jax import lax

NB = 512
KB = 8
RT_DEV = 4
CT_DEV = 25
MT = 64
M = 32768
CT = 400
N = 204800
N_PCOL = 16


def draw_tile_owner(key, part):
    key = jax.random.fold_in(key, 3)
    grid_rows = MT // RT_DEV
    anchor = jax.random.randint(key, (), 0, grid_rows, dtype=jnp.int32)
    return jnp.mod(jnp.arange(MT, dtype=jnp.int32) + anchor, grid_rows)


def draw_inverses(key, part):
    key = jax.random.fold_in(key, 7)
    noise = jax.random.normal(key, (KB, NB, NB), jnp.float32)
    row_index = jnp.arange(NB)[:, None]
    col_index = jnp.arange(NB)[None, :]
    blocks = jnp.where(row_index > col_index, noise * (0.5 / math.sqrt(NB)), 0.0)
    blocks = blocks + jnp.where(row_index == col_index, 1.0, 0.0)
    return blocks.reshape(KB * NB, NB).astype(jnp.bfloat16)


def plant(array, key, least, largest):
    shape = array.shape
    index_at = [jax.random.randint(jax.random.fold_in(key, axis), (), 0, shape[axis]) for axis in range(len(shape))]
    array = array.at[tuple(index_at)].set(least)
    longest = shape.index(max(shape))
    index_at[longest] = (index_at[longest] + 1) % shape[longest]
    return array.at[tuple(index_at)].set(largest)


def levels(rng, extent, split, least, high):
    factor_of = 1.0
    for position, parts in split:
        steps = jax.random.uniform(jax.random.fold_in(jax.random.fold_in(rng, 6), position), (parts,), jnp.float32, least / len(split), high / len(split))
        factor_of = factor_of * jnp.repeat(jnp.exp(steps), extent[position] // parts).reshape((-1,) + (1,) * (len(extent) - 1 - position))
    return factor_of


def bell_draw(rng, extent, width, reach, cuts=(), kind=jnp.bfloat16):
    values = jax.random.normal(rng, extent, jnp.float32) * width
    if len(cuts) > 0:
        values = levels(rng, extent, cuts, -0.22, 0.18) * values
    return jnp.clip(values, min=-reach, max=reach).astype(kind)


def setup_inputs(seed: int = 0) -> dict:
    key_list = jax.random.split(jax.random.key(seed), 8)
    seeds = plant(jax.random.randint(key_list[0], (MT, CT), 0, 1073741824), jax.random.fold_in(key_list[0], 1), 0, 1073741823).astype(jnp.int32)
    tile_owner = draw_tile_owner(jax.random.fold_in(key_list[7], 71), 0)
    vector = bell_draw(key_list[2], (N,), 1.0, 6.0, ((0, 256),), jnp.float32)
    rhs = bell_draw(key_list[3], (M,), 1.0, 6.0, ((0, 16),), jnp.float32)
    panel = bell_draw(key_list[4], (M, KB * NB), NB ** -0.5, 0.25, ((0, 16), (1, 16)))
    tile_scales = jnp.clip(jnp.exp(math.log(0.5) - 1.609438 * jax.random.uniform(key_list[5], (MT, KB), jnp.float32) ** levels(key_list[5], (MT, KB), ((0, 16),), -0.2, 0.2)), 0.1, 0.5)
    inverses = draw_inverses(jax.random.fold_in(key_list[7], 71), 0)
    return dict(seeds=seeds, tile_owner=tile_owner, vector=vector, rhs=rhs, panel=panel, tile_scales=tile_scales, inverses=inverses)


def scramble(offsets, seed_values):
    mixed = offsets * jnp.int32(1103515245) + seed_values
    mixed = mixed ^ lax.shift_right_logical(mixed, jnp.int32(15))
    mixed = mixed * jnp.int32(747796405)
    mixed = mixed ^ lax.shift_right_logical(mixed, jnp.int32(13))
    mixed = mixed * jnp.int32(1274126177)
    mixed = mixed ^ lax.shift_right_logical(mixed, jnp.int32(16))
    return lax.shift_right_logical(mixed, jnp.int32(8)).astype(jnp.float32) * (2.0 ** -32) - 2.0 ** -9


def make_tiles(seed_cols, row_tiles, col_global):
    inner = jnp.arange(NB, dtype=jnp.int32)
    offsets = inner[:, None] * NB + jnp.mod(col_global, NB)[None, :]
    values = scramble(offsets[None, :, :], seed_cols[:, None, :])
    row_global = row_tiles[:, None] * NB + inner[None, :]
    on_diag = row_global[:, :, None] == col_global[None, None, :]
    values = jnp.where(on_diag, values + 1.0, values)
    return values.reshape(-1, col_global.shape[0])


def reference(seeds, tile_owner, vector, rhs, panel, tile_scales, inverses):
    grid_rows = MT // RT_DEV
    anchor = tile_owner[0]
    slots = jnp.arange(MT, dtype=jnp.int32)
    tile_of_slot = (slots % RT_DEV) * grid_rows + jnp.mod(slots // RT_DEV - anchor, grid_rows)

    def column_step(column_slot, running):
        column_slot = column_slot.astype(jnp.int32)
        tile_col = (column_slot % CT_DEV) * N_PCOL + column_slot // CT_DEV
        col_global = tile_col * NB + jnp.arange(NB, dtype=jnp.int32)
        seed_cols = jnp.broadcast_to(lax.dynamic_slice_in_dim(seeds, column_slot, 1, 1), (MT, NB))
        block = make_tiles(seed_cols, tile_of_slot, col_global)
        pieces = lax.dynamic_slice_in_dim(vector, column_slot * NB, NB)
        return running + jnp.dot(block, pieces, precision=lax.Precision.HIGHEST, preferred_element_type=jnp.float32)

    product = lax.fori_loop(0, CT, column_step, jnp.zeros((M,), jnp.float32))
    current = rhs - product
    panel_wide = panel.astype(jnp.float32)
    solved_blocks = []
    for block_col in range(KB):
        slot = tile_owner[block_col] * RT_DEV + block_col // grid_rows
        diag_rows = lax.dynamic_slice_in_dim(current, slot * NB, NB)
        inverse = inverses[block_col * NB:(block_col + 1) * NB].astype(jnp.float32)
        solution = jnp.dot(inverse, diag_rows, precision=lax.Precision.HIGHEST, preferred_element_type=jnp.float32)
        update = jnp.dot(panel_wide[:, block_col * NB:(block_col + 1) * NB], solution,
                         precision=lax.Precision.HIGHEST, preferred_element_type=jnp.float32).reshape(MT, NB)
        factor = jnp.where(tile_of_slot > block_col, tile_scales[:, block_col], jnp.float32(0.0))
        current = current - (update * factor[:, None]).reshape(M)
        solved_blocks.append(solution)
    return jnp.concatenate(solved_blocks), current
```

```python
import functools

import jax
import jax.numpy as jnp
from jax import lax
from jax.experimental import pallas as pl
from jax.experimental.pallas import tpu as pltpu
from jax.sharding import PartitionSpec as P

NB = 512
KB = 8
RT_DEV = 4
CT_DEV = 25
GRID = 16
ROWS = RT_DEV * NB
LANES = 128
GROUPS = NB // LANES
STRIP = 32
UNIT = 2.0 ** -40

VMEM = pl.BlockSpec(memory_space=pltpu.VMEM)
SMEM = pl.BlockSpec(memory_space=pltpu.SMEM)
BIG = 48 * 1024 * 1024


def shift_right(value, amount):
    return lax.shift_right_logical(value, jnp.full_like(value, amount))


def signed_hash(mixed):
    mixed = mixed ^ shift_right(mixed, 15)
    mixed = mixed * jnp.int32(747796405)
    mixed = mixed ^ shift_right(mixed, 13)
    mixed = mixed * jnp.int32(1274126177)
    return (mixed ^ jnp.int32(-2147483648)) ^ shift_right(mixed, 16)


def hash_kernel(first_row, rows, with_sum, seeds, v, acc_out, *sum_out):
    slot = lax.axis_index("prow") * RT_DEV
    bias = jnp.sum(v[...], axis=0, keepdims=True) * jnp.float32(-127.5)

    def strip(number, carry):
        row = first_row + number * STRIP
        tile = row // NB
        inner = row % NB
        t = (inner + lax.broadcasted_iota(jnp.int32, (STRIP, LANES), 0)) * jnp.int32(NB)
        u = lax.broadcasted_iota(jnp.int32, (STRIP, LANES), 1)
        base = [(t + u + jnp.int32(LANES * g)) * jnp.int32(1103515245) for g in range(GROUPS)]
        accs = [jnp.zeros((STRIP, LANES), jnp.float32) for _ in range(GROUPS)]
        accs[0] = accs[0] + bias
        for j in range(CT_DEV):
            seed = seeds[slot + tile, j]
            for g in range(GROUPS):
                entries = jnp.broadcast_to(v[pl.ds(GROUPS * j + g, 1), :], (STRIP, LANES))
                accs[g] = accs[g] + signed_hash(base[g] + seed).astype(jnp.float32) * entries
        total = (accs[0] + accs[1]) + (accs[2] + accs[3])
        acc_out[pl.ds(pl.multiple_of(number * STRIP, STRIP), STRIP), :] = total
        return carry

    lax.fori_loop(0, rows // STRIP, strip, 0)
    if with_sum:
        sum_out[0][...] = jnp.sum(acc_out[...].T, axis=0, keepdims=True)


def hash_rows(seeds, v, first_row, rows, with_sum=False):
    shapes = [jax.ShapeDtypeStruct((rows, LANES), jnp.float32)]
    if with_sum:
        shapes.append(jax.ShapeDtypeStruct((1, rows), jnp.float32))
    work = rows * CT_DEV * NB
    return pl.pallas_call(
        functools.partial(hash_kernel, first_row, rows, with_sum),
        out_shape=shapes,
        in_specs=[SMEM, VMEM],
        out_specs=[VMEM] * len(shapes),
        cost_estimate=pl.CostEstimate(flops=work * 14, bytes_accessed=rows * LANES * 4, transcendentals=0),
        name=f"hash_{first_row}",
    )(seeds, v)


def step_kernel(k, residual, *refs):
    if k == 0:
        inv, tiles, total_out, solved_out = refs
    else:
        same, other, solved_in, inv, tiles, total_out, solved_out = refs
    col = lax.axis_index("pcol")
    mine = col // 2 == k

    @pl.when(mine)
    def _():
        s = residual[...]
        if k > 0:
            running = same[...] + other[...]
            s = s - running[k:k + 1, :]
        y = jnp.sum(inv[...].astype(jnp.float32) * s, axis=1, keepdims=True)
        eye = lax.broadcasted_iota(jnp.int32, (256, 256), 0) == lax.broadcasted_iota(jnp.int32, (256, 256), 1)
        solved_out[...] = jnp.sum(jnp.where(eye, y, 0.0), axis=0, keepdims=True)
        if k < KB - 1:
            rows = [jnp.zeros((1, NB), jnp.float32)] * (k + 1)
            for kk in range(k + 1, KB):
                part = jnp.zeros((16, NB), jnp.float32)
                for j in range(GRID):
                    part = part + tiles[j, kk - 1] * y[16 * j:16 * j + 16]
                rows.append(jnp.sum(part, axis=0, keepdims=True))
            update = jnp.concatenate(rows, axis=0)
            if k > 0:
                update = update + jnp.where(col % 2 == 0, running, 0.0)
            total_out[...] = update

    @pl.when(jnp.logical_not(mine))
    def _():
        if k > 0:
            solved_out[...] = solved_in[...]
        else:
            solved_out[...] = jnp.zeros_like(solved_out)
        if k < KB - 1:
            total_out[...] = jnp.zeros_like(total_out)


def step(k, residual, running, solved, inv, tiles):
    args = (residual,) if k == 0 else (residual, running[0], running[1], solved)
    return pl.pallas_call(
        functools.partial(step_kernel, k),
        out_shape=[jax.ShapeDtypeStruct((KB, NB), jnp.float32), jax.ShapeDtypeStruct((1, 256), jnp.float32)],
        in_specs=[VMEM] * (len(args) + 2),
        out_specs=[VMEM] * 2,
        compiler_params=pltpu.CompilerParams(vmem_limit_bytes=BIG),
        name=f"step_{k}",
    )(*args, inv, tiles)


def last_kernel(count, factor, solved, panel, *refs):
    accs, out = refs[:count], refs[count]
    y = solved[...]
    row = 0
    for acc in accs:
        rows = acc.shape[0]
        for at in range(0, rows, LANES):
            part = panel[row + at:row + at + LANES, :].astype(jnp.float32) * y
            part = (part[:, :LANES] + part[:, LANES:]) * factor[(row + at) // NB]
            part = part + acc[at:at + LANES, :] * jnp.float32(UNIT)
            out[(row + at) // LANES, :] = jnp.sum(part.T, axis=0)
        row += rows


def last(factor, solved, panel, accs):
    return pl.pallas_call(
        functools.partial(last_kernel, len(accs)),
        out_shape=jax.ShapeDtypeStruct((GRID, LANES), jnp.float32),
        in_specs=[SMEM] + [VMEM] * (2 + len(accs)),
        out_specs=VMEM,
        compiler_params=pltpu.CompilerParams(vmem_limit_bytes=BIG),
        name="last",
    )(factor, solved, panel, *accs)


def to_all(value, axis):
    return lax.all_to_all(jnp.broadcast_to(value[None], (GRID,) + value.shape), axis, 0, 0, tiled=True)


def after(value, *others):
    return lax.optimization_barrier((value,) + others)[0]


def body(seeds, tile_owner, vector, rhs, panel, tile_scales, inverses):
    row_index = lax.axis_index("prow")
    col_index = lax.axis_index("pcol")
    anchor = tile_owner[0]
    block = col_index // 2
    first_tile = jnp.mod(row_index - anchor, GRID)
    my_tiles = jnp.arange(RT_DEV, dtype=jnp.int32) * GRID + first_tile
    scales = lax.dynamic_slice_in_dim(tile_scales, block, 1, 1)[:, 0]
    factor = jnp.where(my_tiles > block, scales, jnp.float32(0.0))

    v = to_all(vector, "prow").reshape(CT_DEV * GROUPS, LANES)
    scaled = (panel[:NB].astype(jnp.float32) * factor[0]).T.reshape(GRID, GRID, NB)
    spread = lax.all_to_all(scaled, "prow", 0, 0, tiled=True)
    own = lax.dynamic_slice_in_dim(jnp.concatenate([spread, spread]), anchor + 1, KB - 1, 0)
    tiles = to_all(own, "prow")

    acc0, sum0 = hash_rows(seeds, v, 0, NB, True)
    entries = jnp.where(first_tile == col_index, v.reshape(CT_DEV, NB)[:RT_DEV].reshape(ROWS), 0.0)
    given = jnp.where(col_index == 0, rhs, 0.0) - entries

    part = given[:NB] - sum0[0] * jnp.float32(UNIT)
    gathered = to_all(part, "prow")
    acc1 = hash_rows(seeds, after(v, part), NB, 384)[0]
    blocks = lax.dynamic_slice_in_dim(jnp.concatenate([gathered, gathered]), anchor, KB, 0)
    blocks = after(jnp.repeat(blocks, 2, axis=0), acc1)
    parts = lax.all_to_all(blocks, "pcol", 0, 0, tiled=True)
    acc2 = hash_rows(seeds, after(v, blocks), NB + 384, 384)[0]
    residual = after(jnp.sum(parts, axis=0, keepdims=True), acc2)

    accs = [acc0, acc1, acc2]
    running, solved = None, None
    row = NB + 768
    for k in range(KB):
        total, solved = step(k, residual, running, solved, inverses, tiles)
        if k == KB - 1:
            break
        same = lax.ppermute(total, "pcol", [(2 * k + h, 2 * k + 2 + h) for h in range(2)])
        other = lax.ppermute(total, "pcol", [(2 * k + h, 2 * k + 3 - h) for h in range(2)])
        if row < ROWS:
            accs.append(hash_rows(seeds, after(v, total), row, 128)[0])
            row += 128
            same = after(same, accs[-1])
        running = (same, other)

    sums = given.reshape(GRID, LANES) - last(factor, solved, panel, accs)
    updated = jnp.sum(lax.all_to_all(sums, "pcol", 0, 0, tiled=True), axis=0)
    return (solved.reshape(256), updated)


def solution(mesh):
    placed = (
        P(None, "pcol"),
        P(),
        P(("pcol", "prow")),
        P("prow"),
        P("prow", "pcol"),
        P("prow", None),
        P("pcol", None),
    )
    return jax.shard_map(
        body,
        mesh=mesh,
        in_specs=placed,
        out_specs=(P("pcol"), P(("prow", "pcol"))),
        check_vma=False,
    )
```

```python
import functools

import jax
import jax.numpy as jnp
from jax import lax
from jax.experimental import pallas as pl
from jax.experimental.pallas import tpu as pltpu
from jax.sharding import PartitionSpec as P

NB = 512
KB = 8
RT_DEV = 4
CT_DEV = 25
GRID = 16
ROWS = RT_DEV * NB
LANES = 128
GROUPS = NB // LANES
STRIP = 32
UNIT = 2.0 ** -40
NEAR = 4
PIECE = 256
WIDE = 64
WINDOW = 7
AHEAD = 2
GAPS = (1, 3, 4, 5)
BIAS = -127.5

VMEM = pl.BlockSpec(memory_space=pltpu.VMEM)
SMEM = pl.BlockSpec(memory_space=pltpu.SMEM)
LIMIT = pltpu.CompilerParams(vmem_limit_bytes=10 * 1024 * 1024)


def shift_right(value, amount):
    return lax.shift_right_logical(value, jnp.full_like(value, amount))


def signed_hash(mixed):
    mixed = mixed ^ shift_right(mixed, 15)
    mixed = mixed * jnp.int32(747796405)
    mixed = mixed ^ shift_right(mixed, 13)
    mixed = mixed * jnp.int32(1274126177)
    return (mixed ^ jnp.int32(-2147483648)) ^ shift_right(mixed, 16)


def weighted(bases, seed, entries, sums):
    return [
        total + signed_hash(base + seed).astype(jnp.float32) * entry
        for base, entry, total in zip(bases, entries, sums)
    ]


def first_kernel(owner, seeds, window, rhs, vector, out, sums):
    row_index, col_index = lax.axis_index("prow"), lax.axis_index("pcol")
    anchor = owner[0]
    my_tile = (row_index - anchor + GRID) & (GRID - 1)
    group = (row_index * 25) >> 2
    bias = jnp.broadcast_to(jnp.sum(window[...], axis=0, keepdims=True) * jnp.float32(BIAS), (WIDE, LANES))
    u = lax.broadcasted_iota(jnp.int32, (WIDE, LANES), 1)
    t = lax.broadcasted_iota(jnp.int32, (WIDE, LANES), 0)

    def tile(k, carry):
        slot = ((anchor + k) & (GRID - 1)) * RT_DEV
        shifts = [
            seeds[slot, (group + i) >> 2] + (((group + i) & 3) * LANES) * jnp.int32(1103515245)
            for i in range(WINDOW)
        ]

        def strip(number, inner):
            base = ((number * WIDE + t) * NB + u) * jnp.int32(1103515245)
            totals = [bias, jnp.zeros((WIDE, LANES), jnp.float32)]
            for i in range(WINDOW):
                entries = jnp.broadcast_to(window[i:i + 1, :], (WIDE, LANES))
                totals[i % 2] = weighted([base], shifts[i], [entries], [totals[i % 2]])[0]
            sums[pl.ds(pl.multiple_of(number * WIDE, WIDE), WIDE), :] = totals[0] + totals[1]
            return inner

        lax.fori_loop(0, NB // WIDE, strip, 0)
        value = jnp.sum(sums[...].T, axis=0, keepdims=True) * jnp.float32(-UNIT)
        value = value + jnp.where((col_index == 0) & (k == my_tile), rhs[...], 0.0)
        value = value - jnp.where((row_index == 0) & (col_index == k), vector[...], 0.0)
        out[pl.ds(2 * k, 2), :, :] = jnp.broadcast_to(value[None], (2, 1, NB))
        return carry

    lax.fori_loop(0, KB, tile, 0)


def first_rows(tile_owner, seeds, window, rhs, vector):
    return pl.pallas_call(
        first_kernel,
        out_shape=jax.ShapeDtypeStruct((GRID, 1, NB), jnp.float32),
        in_specs=[SMEM, SMEM, VMEM, VMEM, VMEM],
        out_specs=VMEM,
        scratch_shapes=[pltpu.VMEM((NB, LANES), jnp.float32)],
        cost_estimate=pl.CostEstimate(flops=KB * NB * 1600, bytes_accessed=GRID * NB * 4, transcendentals=0),
        compiler_params=LIMIT,
        name="first_rows",
    )(tile_owner, seeds, window, rhs, vector)


def hash_kernel(tile, start, with_sum, seeds, meta, v, *outs):
    acc_out = outs[0]
    bias = jnp.sum(jnp.sum(v[...], axis=0), axis=0, keepdims=True) * jnp.float32(BIAS)
    begin = meta[0] if with_sum else start

    def strip(number, carry):
        inner = begin + number * STRIP
        t = (inner + lax.broadcasted_iota(jnp.int32, (STRIP, LANES), 0)) * jnp.int32(NB)
        u = lax.broadcasted_iota(jnp.int32, (STRIP, LANES), 1)
        bases = [(t + u + jnp.int32(LANES * g)) * jnp.int32(1103515245) for g in range(GROUPS)]
        sums = [jnp.broadcast_to(bias, (STRIP, LANES))] + [jnp.zeros((STRIP, LANES), jnp.float32)] * (GROUPS - 1)
        for j in range(CT_DEV):
            entries = [jnp.broadcast_to(v[j, g:g + 1, :], (STRIP, LANES)) for g in range(GROUPS)]
            sums = weighted(bases, seeds[tile, j], entries, sums)
        total = (sums[0] + sums[1]) + (sums[2] + sums[3])
        acc_out[pl.ds(pl.multiple_of(number * STRIP, STRIP), STRIP), :] = total
        return carry

    lax.fori_loop(0, PIECE // STRIP, strip, 0)
    if with_sum:
        outs[1][...] = jnp.sum(acc_out[...].T, axis=0, keepdims=True)


def hash_rows(seeds, meta, v, tile, start, with_sum=False):
    shapes = [jax.ShapeDtypeStruct((PIECE, LANES), jnp.float32)]
    if with_sum:
        shapes.append(jax.ShapeDtypeStruct((1, PIECE), jnp.float32))
    return pl.pallas_call(
        functools.partial(hash_kernel, tile, start, with_sum),
        out_shape=shapes,
        in_specs=[SMEM, SMEM, VMEM],
        out_specs=[VMEM] * len(shapes),
        cost_estimate=pl.CostEstimate(
            flops=PIECE * CT_DEV * NB * 2, bytes_accessed=PIECE * LANES * 4, transcendentals=0
        ),
        compiler_params=LIMIT,
        name=f"hash_{tile}_{start}",
    )(seeds, meta, v)


def step_kernel(k, residual, *refs):
    refs = list(refs)
    same, other, solved_in = [refs.pop(0) for _ in range(3)] if k > 0 else [None] * 3
    inv = refs.pop(0)
    near, far = refs[:4], refs[4:8]
    total_out, solved_out, spread_y = refs[8:]
    col = lax.axis_index("pcol")
    me = lax.axis_index("prow")
    mine = col // 2 == k

    @pl.when(mine)
    def _():
        s = residual[...]
        if k > 0:
            running = same[...] + other[...]
            s = s - running[k:k + 1, :]
        y = jnp.sum(inv[...].astype(jnp.float32) * s, axis=1, keepdims=True)
        if k < KB - 1:
            spread_y[...] = jnp.broadcast_to(y, (256, LANES)).reshape(GRID, 16, LANES)
            rows = [jnp.zeros((1, NB), jnp.float32)] * (k + 1)
            for kk in range(k, KB - 1):
                part = jnp.zeros((16, NB), jnp.float32)
                for m in range(4):
                    for i in range(4):
                        if kk < NEAR:
                            tile, source = near[m][i, kk], me ^ (4 * m + i)
                        else:
                            tile, source = far[m][i, kk - NEAR], me ^ (4 * i + m)
                        part = part + tile * jnp.concatenate([spread_y[source]] * GROUPS, axis=1)
                rows.append(jnp.sum(part, axis=0, keepdims=True))
            update = jnp.concatenate(rows, axis=0)
            if k > 0:
                update = update + jnp.where(col % 2 == 0, running, 0.0)
            total_out[...] = update
        eye = lax.broadcasted_iota(jnp.int32, (256, 256), 0) == lax.broadcasted_iota(jnp.int32, (256, 256), 1)
        solved_out[...] = jnp.sum(jnp.where(eye, y, 0.0), axis=0, keepdims=True)

    @pl.when(jnp.logical_not(mine))
    def _():
        if k > 0:
            solved_out[...] = solved_in[...]
        else:
            solved_out[...] = jnp.zeros_like(solved_out)
        if k < KB - 1:
            total_out[...] = jnp.zeros_like(total_out)


def step(k, residual, running, solved, inv, tiles):
    args = (residual,) if k == 0 else (residual, running[0], running[1], solved)
    return pl.pallas_call(
        functools.partial(step_kernel, k),
        out_shape=[jax.ShapeDtypeStruct((KB, NB), jnp.float32), jax.ShapeDtypeStruct((1, 256), jnp.float32)],
        in_specs=[VMEM] * (len(args) + 9),
        out_specs=[VMEM] * 2,
        scratch_shapes=[pltpu.VMEM((GRID, 16, LANES), jnp.float32)],
        compiler_params=LIMIT,
        name=f"step_{k}",
    )(*args, inv, *tiles)


def last_kernel(factor, owner, rhs, v, residual, own_sum, their_sum, solved, panel, *refs):
    accs, out = refs[:-1], refs[-1]
    row_index, col_index = lax.axis_index("prow"), lax.axis_index("pcol")
    my_tile = (row_index - owner[0] + GRID) & (GRID - 1)
    early = my_tile < KB
    y = solved[...]
    for at in range(0, ROWS, LANES):
        n = at // LANES
        part = panel[at:at + LANES, :].astype(jnp.float32) * y
        part = (part[:, :LANES] + part[:, LANES:]) * factor[at // NB]
        if at >= NB:
            piece, row = divmod(at - NB, PIECE)
            part = part + accs[piece][row:row + LANES, :] * jnp.float32(UNIT)
        total = jnp.sum(part.T, axis=0, keepdims=True)
        given = jnp.where(col_index == 0, rhs[n:n + 1, :], 0.0)
        given = given - jnp.where(my_tile == col_index, v[n // GROUPS, n % GROUPS:n % GROUPS + 1, :], 0.0)
        if at < NB:
            held = own_sum if at < PIECE else their_sum
            given = given - held[:, at % PIECE:at % PIECE + LANES] * jnp.float32(UNIT)
            known = jnp.where(col_index == 2 * my_tile, residual[:, at:at + LANES], 0.0)
            given = jnp.where(early, known, given)
        out[n:n + 1, :] = given - total


def last(factor, owner, rhs, v, residual, own_sum, their_sum, solved, panel, accs):
    return pl.pallas_call(
        last_kernel,
        out_shape=jax.ShapeDtypeStruct((GRID, LANES), jnp.float32),
        in_specs=[SMEM] * 2 + [VMEM] * (7 + len(accs)),
        out_specs=VMEM,
        compiler_params=LIMIT,
        name="last",
    )(factor, owner, rhs, v, residual, own_sum, their_sum, solved, panel, *accs)


def to_all(value, axis):
    return lax.all_to_all(jnp.broadcast_to(value[None], (GRID,) + value.shape), axis, 0, 0, tiled=True)


def exchange(value, mask):
    return lax.ppermute(value, "prow", [(i, i ^ mask) for i in range(GRID)])


def after(value, *others):
    return lax.optimization_barrier((value,) + others)[0]


def body(seeds, tile_owner, vector, rhs, panel, tile_scales, inverses):
    row_index = lax.axis_index("prow")
    col_index = lax.axis_index("pcol")
    anchor = tile_owner[0]
    block = col_index // 2
    first_tile = jnp.mod(row_index - anchor, GRID)
    my_tiles = jnp.arange(RT_DEV, dtype=jnp.int32) * GRID + first_tile
    scales = lax.dynamic_slice_in_dim(tile_scales, block, 1, 1)[:, 0]
    factor = jnp.where(my_tiles > block, scales, jnp.float32(0.0))

    scaled = (panel[:NB].astype(jnp.float32) * factor[0]).T.reshape(GRID, 16, NB)
    padded = jnp.pad(vector, (0, 2 * NB - vector.shape[0])).reshape(1, 2, NB)
    sent = jnp.concatenate([scaled, jnp.broadcast_to(padded, (GRID, 2, NB))], axis=1)
    came = lax.all_to_all(sent, "prow", 0, 0, tiled=True)

    edge = jnp.zeros((96,), jnp.float32)
    window = lax.dynamic_slice_in_dim(
        jnp.concatenate([edge, vector, edge]), 96 - 32 * jnp.mod(row_index, 4), WINDOW * LANES, 0
    ).reshape(WINDOW, LANES)
    parts = first_rows(
        tile_owner, seeds, window, rhs[:NB].reshape(1, NB), vector[:NB].reshape(1, NB)
    )

    early = first_tile < KB
    shared = jnp.where(early, jnp.mod(row_index + KB, GRID), row_index) * RT_DEV
    seed_rows = jnp.concatenate([
        lax.dynamic_slice_in_dim(seeds, row_index * RT_DEV + 1, RT_DEV - 1, 0),
        lax.dynamic_slice_in_dim(seeds, shared, 1, 0),
    ])
    meta = jnp.where(early, PIECE, 0).reshape(1)

    own = lax.dynamic_slice_in_dim(jnp.concatenate([came, came])[:, :16], anchor + 1, KB - 1, 0)
    v = came[:, 16:].reshape(GRID, 2 * NB)[:, :vector.shape[0]].reshape(CT_DEV, GROUPS, LANES)
    near, far, parts, v = lax.optimization_barrier((own[:NEAR], own[NEAR:], parts, v))
    near = jnp.stack([near] + [exchange(near, m) for m in (1, 2, 3)])
    far = jnp.stack([far] + [exchange(far, m) for m in (4, 8, 12)])
    accs = []
    _, own_sum = hash_rows(seed_rows, meta, v, RT_DEV - 1, 0, True)
    their_sum = exchange(own_sum, KB)
    part = jnp.sum(lax.all_to_all(parts, "pcol", 0, 0, tiled=True), axis=0)
    near, far, part, own_sum = lax.optimization_barrier((near, far, part, own_sum))
    tiles = [near] + [exchange(near, m) for m in (4, 8, 12)] + [far] + [exchange(far, m) for m in (1, 2, 3)]
    came = to_all(part, "prow")
    here = after(v, part)
    for n in range(AHEAD):
        accs.append(hash_rows(seed_rows, meta, here, *divmod(n * PIECE, NB))[0])
        here = after(v, accs[-1])
    residual = after(jnp.sum(came, axis=0), accs[-1])

    running, solved = None, None
    for k in range(KB):
        total, solved = step(k, residual, running, solved, inverses, tiles)
        if k == KB - 1:
            break
        same = lax.ppermute(total, "pcol", [(2 * k + h, 2 * k + 2 + h) for h in range(2)])
        other = lax.ppermute(total, "pcol", [(2 * k + h, 2 * k + 3 - h) for h in range(2)])
        if k in GAPS:
            accs.append(hash_rows(seed_rows, meta, after(v, total), *divmod(len(accs) * PIECE, NB))[0])
            same = after(same, accs[-1])
        running = (same, other)

    sums = last(
        factor, tile_owner, rhs.reshape(GRID, LANES), v, residual, own_sum, their_sum, solved, panel, accs
    )
    updated = jnp.sum(lax.all_to_all(sums, "pcol", 0, 0, tiled=True), axis=0)
    return (solved.reshape(256), updated)


def solution(mesh):
    placed = (
        P(None, "pcol"),
        P(),
        P(("pcol", "prow")),
        P("prow"),
        P("prow", "pcol"),
        P("prow", None),
        P("pcol", None),
    )
    return jax.shard_map(
        body,
        mesh=mesh,
        in_specs=placed,
        out_specs=(P("pcol"), P(("prow", "pcol"))),
        check_vma=False,
    )
```

```python
import functools

import jax
import jax.numpy as jnp
from jax import lax
from jax.experimental import pallas as pl
from jax.experimental.pallas import tpu as pltpu
from jax.sharding import PartitionSpec as P

NB = 512
KB = 8
RT_DEV = 4
CT_DEV = 25
GRID = 16
ROWS = RT_DEV * NB
LANES = 128
GROUPS = NB // LANES
STRIP = 32
UNIT = 2.0 ** -40
NEAR = 4
PIECE = 256
WIDE = 64
WINDOW = 7
AHEAD = 2
GAPS = (1, 2, 3, 4)
BIAS = -127.5

VMEM = pl.BlockSpec(memory_space=pltpu.VMEM)
ANY = pl.BlockSpec(memory_space=pl.ANY)
SMEM = pl.BlockSpec(memory_space=pltpu.SMEM)
LIMIT = pltpu.CompilerParams(vmem_limit_bytes=6 * 1024 * 1024)


def shift_right(value, amount):
    return lax.shift_right_logical(value, jnp.full_like(value, amount))


def signed_hash(mixed):
    mixed = mixed ^ shift_right(mixed, 15)
    mixed = mixed * jnp.int32(747796405)
    mixed = mixed ^ shift_right(mixed, 13)
    mixed = mixed * jnp.int32(1274126177)
    return (mixed ^ jnp.int32(-2147483648)) ^ shift_right(mixed, 16)


def weighted(bases, seed, entries, sums):
    return [
        total + signed_hash(base + seed).astype(jnp.float32) * entry
        for base, entry, total in zip(bases, entries, sums)
    ]


def first_kernel(owner, seeds, window, rhs, vector, out, sums):
    row_index, col_index = lax.axis_index("prow"), lax.axis_index("pcol")
    anchor = owner[0]
    my_tile = (row_index - anchor + GRID) & (GRID - 1)
    group = (row_index * 25) >> 2
    bias = jnp.broadcast_to(jnp.sum(window[...], axis=0, keepdims=True) * jnp.float32(BIAS), (WIDE, LANES))
    u = lax.broadcasted_iota(jnp.int32, (WIDE, LANES), 1)
    t = lax.broadcasted_iota(jnp.int32, (WIDE, LANES), 0)

    def tile(k, carry):
        slot = ((anchor + k) & (GRID - 1)) * RT_DEV
        shifts = [
            seeds[slot, (group + i) >> 2] + (((group + i) & 3) * LANES) * jnp.int32(1103515245)
            for i in range(WINDOW)
        ]

        def strip(number, inner):
            base = ((number * WIDE + t) * NB + u) * jnp.int32(1103515245)
            totals = [bias, jnp.zeros((WIDE, LANES), jnp.float32)]
            for i in range(WINDOW):
                entries = jnp.broadcast_to(window[i:i + 1, :], (WIDE, LANES))
                totals[i % 2] = weighted([base], shifts[i], [entries], [totals[i % 2]])[0]
            sums[pl.ds(pl.multiple_of(number * WIDE, WIDE), WIDE), :] = totals[0] + totals[1]
            return inner

        lax.fori_loop(0, NB // WIDE, strip, 0)
        value = jnp.sum(sums[...].T, axis=0, keepdims=True) * jnp.float32(-UNIT)
        value = value + jnp.where((col_index == 0) & (k == my_tile), rhs[...], 0.0)
        value = value - jnp.where((row_index == 0) & (col_index == k), vector[...], 0.0)
        out[pl.ds(2 * k, 2), :, :] = jnp.broadcast_to(value[None], (2, 1, NB))
        return carry

    lax.fori_loop(0, KB, tile, 0)


def first_rows(tile_owner, seeds, window, rhs, vector):
    return pl.pallas_call(
        first_kernel,
        out_shape=jax.ShapeDtypeStruct((GRID, 1, NB), jnp.float32),
        in_specs=[SMEM, SMEM, VMEM, VMEM, VMEM],
        out_specs=VMEM,
        scratch_shapes=[pltpu.VMEM((NB, LANES), jnp.float32)],
        cost_estimate=pl.CostEstimate(flops=KB * NB * 1600, bytes_accessed=GRID * NB * 4, transcendentals=0),
        compiler_params=LIMIT,
        name="first_rows",
    )(tile_owner, seeds, window, rhs, vector)


def hash_kernel(row, tile, start, seeds, meta, v, table, _, out, held):
    bias = jnp.sum(jnp.sum(v[...], axis=0), axis=0, keepdims=True) * jnp.float32(BIAS)
    begin = meta[0] if start is None else start

    def strip(number, carry):
        inner = begin + number * STRIP
        t = (inner + lax.broadcasted_iota(jnp.int32, (STRIP, LANES), 0)) * jnp.int32(NB)
        u = lax.broadcasted_iota(jnp.int32, (STRIP, LANES), 1)
        bases = [(t + u + jnp.int32(LANES * g)) * jnp.int32(1103515245) for g in range(GROUPS)]
        sums = [jnp.broadcast_to(bias, (STRIP, LANES))] + [jnp.zeros((STRIP, LANES), jnp.float32)] * (GROUPS - 1)
        for j in range(CT_DEV):
            entries = [jnp.broadcast_to(v[j, g:g + 1, :], (STRIP, LANES)) for g in range(GROUPS)]
            sums = weighted(bases, seeds[tile, j], entries, sums)
        total = (sums[0] + sums[1]) + (sums[2] + sums[3])
        held[pl.ds(pl.multiple_of(number * STRIP, STRIP), STRIP), :] = total
        return carry

    lax.fori_loop(0, PIECE // STRIP, strip, 0)
    out[...] = table[...]
    out[row:row + 1, :] = jnp.sum(held[...].T, axis=0, keepdims=True) * jnp.float32(UNIT)


def hash_rows(seeds, meta, v, table, token, row):
    tile, start = divmod((row - 1) * PIECE, NB) if row > 0 else (RT_DEV - 1, None)
    return pl.pallas_call(
        functools.partial(hash_kernel, row, tile, start),
        out_shape=jax.ShapeDtypeStruct((KB, PIECE), jnp.float32),
        in_specs=[SMEM, SMEM, VMEM, VMEM, ANY],
        out_specs=VMEM,
        scratch_shapes=[pltpu.VMEM((PIECE, LANES), jnp.float32)],
        cost_estimate=pl.CostEstimate(
            flops=PIECE * CT_DEV * NB * 2, bytes_accessed=PIECE * LANES * 4, transcendentals=0
        ),
        compiler_params=LIMIT,
        name=f"hash_{row}",
    )(seeds, meta, v, table, token)


def step_kernel(k, residual, *refs):
    refs = list(refs)
    same, other, solved_in = [refs.pop(0) for _ in range(3)] if k > 0 else [None] * 3
    inv = refs.pop(0)
    near, far = refs[:4], refs[4:8]
    _, total_out, solved_out, spread_y, held, sem = refs[8:]
    col = lax.axis_index("pcol")
    me = lax.axis_index("prow")
    mine = col // 2 == k

    @pl.when(mine)
    def _():
        if k < KB - 1:
            fetch = pltpu.make_async_copy(far[3].at[:, max(k - NEAR, 0):], held, sem)
            fetch.start()
        s = residual[...]
        if k > 0:
            running = same[...] + other[...]
            s = s - running[k:k + 1, :]
        y = jnp.sum(inv[...].astype(jnp.float32) * s, axis=1, keepdims=True)
        if k < KB - 1:
            spread_y[...] = jnp.broadcast_to(y, (256, LANES)).reshape(GRID, 16, LANES)
            rows = [jnp.zeros((1, NB), jnp.float32)] * (k + 1)
            for kk in range(k, KB - 1):
                if kk == max(k, NEAR):
                    fetch.wait()
                part = jnp.zeros((16, NB), jnp.float32)
                for m in range(4):
                    for i in range(4):
                        if kk < NEAR:
                            tile, source = near[m][i, kk], me ^ (4 * m + i)
                        elif m < 3:
                            tile, source = far[m][i, kk - NEAR], me ^ (4 * i + m)
                        else:
                            tile, source = held[i, kk - max(k, NEAR)], me ^ (4 * i + m)
                        part = part + tile * jnp.concatenate([spread_y[source]] * GROUPS, axis=1)
                rows.append(jnp.sum(part, axis=0, keepdims=True))
            update = jnp.concatenate(rows, axis=0)
            if k > 0:
                update = update + jnp.where(col % 2 == 0, running, 0.0)
            total_out[...] = update
        eye = lax.broadcasted_iota(jnp.int32, (256, 256), 0) == lax.broadcasted_iota(jnp.int32, (256, 256), 1)
        solved_out[...] = jnp.sum(jnp.where(eye, y, 0.0), axis=0, keepdims=True)

    @pl.when(jnp.logical_not(mine))
    def _():
        if k > 0:
            solved_out[...] = solved_in[...]
        else:
            solved_out[...] = jnp.zeros_like(solved_out)
        if k < KB - 1:
            total_out[...] = jnp.zeros_like(total_out)


def step(k, residual, running, solved, inv, tiles, token):
    args = (residual,) if k == 0 else (residual, running[0], running[1], solved)
    return pl.pallas_call(
        functools.partial(step_kernel, k),
        out_shape=[jax.ShapeDtypeStruct((KB, NB), jnp.float32), jax.ShapeDtypeStruct((1, 256), jnp.float32)],
        in_specs=[VMEM] * (len(args) + 8) + [ANY, VMEM],
        out_specs=[VMEM] * 2,
        scratch_shapes=[
            pltpu.VMEM((GRID, 16, LANES), jnp.float32),
            pltpu.VMEM((4, min(KB - 1 - NEAR, max(KB - 1 - k, 1)), 16, NB), jnp.float32),
            pltpu.SemaphoreType.DMA,
        ],
        compiler_params=LIMIT,
        name=f"step_{k}",
    )(*args, inv, *tiles, token)


def last_kernel(factor, owner, rhs, v, residual, theirs, solved, panel, table, out):
    row_index, col_index = lax.axis_index("prow"), lax.axis_index("pcol")
    my_tile = (row_index - owner[0] + GRID) & (GRID - 1)
    y = solved[...]
    for at in range(0, ROWS, LANES):
        n = at // LANES
        part = panel[at:at + LANES, :].astype(jnp.float32) * y
        part = (part[:, :LANES] + part[:, LANES:]) * factor[at // NB]
        total = jnp.sum(part.T, axis=0, keepdims=True)
        given = jnp.where(col_index == 0, rhs[n:n + 1, :], 0.0)
        given = given - jnp.where(my_tile == col_index, v[n // GROUPS, n % GROUPS:n % GROUPS + 1, :], 0.0)
        if at < NB:
            shared = table[0:1, at:at + LANES] if at < PIECE else theirs[:, at - PIECE:at - PIECE + LANES]
            given = given - shared
            known = jnp.where(col_index == 2 * my_tile, residual[:, at:at + LANES], 0.0)
            given = jnp.where(my_tile < KB, known, given)
        else:
            piece, row = divmod(at - NB, PIECE)
            given = given - table[piece + 1:piece + 2, row:row + LANES]
        out[n:n + 1, :] = given - total


def last(factor, owner, rhs, v, residual, theirs, solved, panel, table):
    return pl.pallas_call(
        last_kernel,
        out_shape=jax.ShapeDtypeStruct((GRID, LANES), jnp.float32),
        in_specs=[SMEM] * 2 + [VMEM] * 7,
        out_specs=VMEM,
        compiler_params=LIMIT,
        name="last",
    )(factor, owner, rhs, v, residual, theirs, solved, panel, table)


def to_all(value, axis):
    return lax.all_to_all(jnp.broadcast_to(value[None], (GRID,) + value.shape), axis, 0, 0, tiled=True)


def exchange(value, mask):
    return lax.ppermute(value, "prow", [(i, i ^ mask) for i in range(GRID)])


def body(seeds, tile_owner, vector, rhs, panel, tile_scales, inverses):
    row_index = lax.axis_index("prow")
    col_index = lax.axis_index("pcol")
    anchor = tile_owner[0]
    block = col_index // 2
    first_tile = jnp.mod(row_index - anchor, GRID)
    my_tiles = jnp.arange(RT_DEV, dtype=jnp.int32) * GRID + first_tile
    scales = lax.dynamic_slice_in_dim(tile_scales, block, 1, 1)[:, 0]
    factor = jnp.where(my_tiles > block, scales, jnp.float32(0.0))

    scaled = (panel[:NB].astype(jnp.float32) * factor[0]).T.reshape(GRID, 16, NB)
    padded = jnp.pad(vector, (0, 2 * NB - vector.shape[0])).reshape(1, 2, NB)
    sent = jnp.concatenate([scaled, jnp.broadcast_to(padded, (GRID, 2, NB))], axis=1)
    came = lax.all_to_all(sent, "prow", 0, 0, tiled=True)

    edge = jnp.zeros((96,), jnp.float32)
    window = lax.dynamic_slice_in_dim(
        jnp.concatenate([edge, vector, edge]), 96 - 32 * jnp.mod(row_index, 4), WINDOW * LANES, 0
    ).reshape(WINDOW, LANES)
    parts = first_rows(
        tile_owner, seeds, window, rhs[:NB].reshape(1, NB), vector[:NB].reshape(1, NB)
    )

    early = first_tile < KB
    shared = jnp.where(early, jnp.mod(row_index + KB, GRID), row_index) * RT_DEV
    seed_rows = jnp.concatenate([
        lax.dynamic_slice_in_dim(seeds, row_index * RT_DEV + 1, RT_DEV - 1, 0),
        lax.dynamic_slice_in_dim(seeds, shared, 1, 0),
    ])
    meta = jnp.where(early, PIECE, 0).reshape(1)

    own = lax.dynamic_slice_in_dim(jnp.concatenate([came, came])[:, :16], anchor + 1, KB - 1, 0)
    v = came[:, 16:].reshape(GRID, 2 * NB)[:, :vector.shape[0]].reshape(CT_DEV, GROUPS, LANES)
    near, far, parts, v = lax.optimization_barrier((own[:NEAR], own[NEAR:], parts, v))
    near = jnp.stack([near] + [exchange(near, m) for m in (1, 2, 3)])
    far = jnp.stack([far] + [exchange(far, m) for m in (4, 8, 12)])
    table = hash_rows(seed_rows, meta, v, jnp.zeros((KB, PIECE), jnp.float32), parts, 0)
    part = jnp.sum(lax.all_to_all(parts, "pcol", 0, 0, tiled=True), axis=0)
    near, far, part, table = lax.optimization_barrier((near, far, part, table))
    first, second = exchange(far, 1), exchange(far, 2)
    across = [exchange(near, m) for m in (4, 8, 12)]
    far, first = lax.optimization_barrier((far, first))
    tiles = [near] + across + [far, first, second, exchange(far, 3)]
    came = to_all(jnp.concatenate([part, jnp.pad(table[:1], ((0, 0), (0, PIECE)))]), "prow")
    row = 1
    for _ in range(AHEAD):
        table = hash_rows(seed_rows, meta, v, table, part, row)
        row += 1
    residual = jnp.sum(came[:, :1], axis=0)
    theirs = lax.dynamic_slice_in_dim(came, jnp.mod(row_index + KB, GRID), 1, 0)[0, 1:, :PIECE]

    running, solved = None, None
    for k in range(KB):
        total, solved = step(k, residual, running, solved, inverses, tiles, table)
        if k == KB - 1:
            break
        same = lax.ppermute(total, "pcol", [(2 * k + h, 2 * k + 2 + h) for h in range(2)])
        other = lax.ppermute(total, "pcol", [(2 * k + h, 2 * k + 3 - h) for h in range(2)])
        if k in GAPS:
            table = hash_rows(seed_rows, meta, v, table, total, row)
            row += 1
        running = (same, other)

    sums = last(factor, tile_owner, rhs.reshape(GRID, LANES), v, residual, theirs, solved, panel, table)
    updated = jnp.sum(lax.all_to_all(sums, "pcol", 0, 0, tiled=True), axis=0)
    return (solved.reshape(256), updated)


def solution(mesh):
    placed = (
        P(None, "pcol"),
        P(),
        P(("pcol", "prow")),
        P("prow"),
        P("prow", "pcol"),
        P("prow", None),
        P("pcol", None),
    )
    return jax.shard_map(
        body,
        mesh=mesh,
        in_specs=placed,
        out_specs=(P("pcol"), P(("prow", "pcol"))),
        check_vma=False,
    )
```

```python
import functools

import jax
import jax.numpy as jnp
from jax import lax
from jax.experimental import pallas as pl
from jax.experimental.pallas import tpu as pltpu
from jax.sharding import PartitionSpec as P

NB = 512
KB = 8
RT_DEV = 4
CT_DEV = 25
GRID = 16
ROWS = RT_DEV * NB
LANES = 128
GROUPS = NB // LANES
STRIP = 32
UNIT = 2.0 ** -40
NEAR = 4
PIECE = 256
WIDE = 64
WINDOW = 7
AHEAD = 2
GAPS = (1, 2, 3, 5)
BIAS = -127.5

VMEM = pl.BlockSpec(memory_space=pltpu.VMEM)
ANY = pl.BlockSpec(memory_space=pl.ANY)
SMEM = pl.BlockSpec(memory_space=pltpu.SMEM)
LIMIT = pltpu.CompilerParams(vmem_limit_bytes=6 * 1024 * 1024)


def shift_right(value, amount):
    return lax.shift_right_logical(value, jnp.full_like(value, amount))


def signed_hash(mixed):
    mixed = mixed ^ shift_right(mixed, 15)
    mixed = mixed * jnp.int32(747796405)
    mixed = mixed ^ shift_right(mixed, 13)
    mixed = mixed * jnp.int32(1274126177)
    return (mixed ^ jnp.int32(-2147483648)) ^ shift_right(mixed, 16)


def weighted(bases, seed, entries, sums):
    return [
        total + signed_hash(base + seed).astype(jnp.float32) * entry
        for base, entry, total in zip(bases, entries, sums)
    ]


def first_kernel(owner, seeds, window, rhs, vector, out, sums):
    row_index, col_index = lax.axis_index("prow"), lax.axis_index("pcol")
    anchor = owner[0]
    my_tile = (row_index - anchor + GRID) & (GRID - 1)
    group = (row_index * 25) >> 2
    bias = jnp.broadcast_to(jnp.sum(window[...], axis=0, keepdims=True) * jnp.float32(BIAS), (WIDE, LANES))
    u = lax.broadcasted_iota(jnp.int32, (WIDE, LANES), 1)
    t = lax.broadcasted_iota(jnp.int32, (WIDE, LANES), 0)

    def tile(k, carry):
        slot = ((anchor + k) & (GRID - 1)) * RT_DEV
        shifts = [
            seeds[slot, (group + i) >> 2] + (((group + i) & 3) * LANES) * jnp.int32(1103515245)
            for i in range(WINDOW)
        ]

        def strip(number, inner):
            base = ((number * WIDE + t) * NB + u) * jnp.int32(1103515245)
            totals = [bias, jnp.zeros((WIDE, LANES), jnp.float32)]
            for i in range(WINDOW):
                entries = jnp.broadcast_to(window[i:i + 1, :], (WIDE, LANES))
                totals[i % 2] = weighted([base], shifts[i], [entries], [totals[i % 2]])[0]
            sums[pl.ds(pl.multiple_of(number * WIDE, WIDE), WIDE), :] = totals[0] + totals[1]
            return inner

        lax.fori_loop(0, NB // WIDE, strip, 0)
        value = jnp.sum(sums[...].T, axis=0, keepdims=True) * jnp.float32(-UNIT)
        value = value + jnp.where((col_index == 0) & (k == my_tile), rhs[...], 0.0)
        value = value - jnp.where((row_index == 0) & (col_index == k), vector[...], 0.0)
        out[pl.ds(2 * k, 2), :, :] = jnp.broadcast_to(value[None], (2, 1, NB))
        return carry

    lax.fori_loop(0, KB, tile, 0)


def first_rows(tile_owner, seeds, window, rhs, vector):
    return pl.pallas_call(
        first_kernel,
        out_shape=jax.ShapeDtypeStruct((GRID, 1, NB), jnp.float32),
        in_specs=[SMEM, SMEM, VMEM, VMEM, VMEM],
        out_specs=VMEM,
        scratch_shapes=[pltpu.VMEM((NB, LANES), jnp.float32)],
        cost_estimate=pl.CostEstimate(flops=KB * NB * 1600, bytes_accessed=GRID * NB * 4, transcendentals=0),
        compiler_params=LIMIT,
        name="first_rows",
    )(tile_owner, seeds, window, rhs, vector)


def hash_kernel(row, tile, start, seeds, meta, v, table, _, out, held):
    bias = jnp.sum(jnp.sum(v[...], axis=0), axis=0, keepdims=True) * jnp.float32(BIAS)
    begin = meta[0] if start is None else start

    def strip(number, carry):
        inner = begin + number * STRIP
        t = (inner + lax.broadcasted_iota(jnp.int32, (STRIP, LANES), 0)) * jnp.int32(NB)
        u = lax.broadcasted_iota(jnp.int32, (STRIP, LANES), 1)
        bases = [(t + u + jnp.int32(LANES * g)) * jnp.int32(1103515245) for g in range(GROUPS)]
        sums = [jnp.broadcast_to(bias, (STRIP, LANES))] + [jnp.zeros((STRIP, LANES), jnp.float32)] * (GROUPS - 1)
        for j in range(CT_DEV):
            entries = [jnp.broadcast_to(v[j, g:g + 1, :], (STRIP, LANES)) for g in range(GROUPS)]
            sums = weighted(bases, seeds[tile, j], entries, sums)
        total = (sums[0] + sums[1]) + (sums[2] + sums[3])
        held[pl.ds(pl.multiple_of(number * STRIP, STRIP), STRIP), :] = total
        return carry

    lax.fori_loop(0, PIECE // STRIP, strip, 0)
    out[...] = table[...]
    out[row:row + 1, :] = jnp.sum(held[...].T, axis=0, keepdims=True) * jnp.float32(UNIT)


def hash_rows(seeds, meta, v, table, token, row):
    tile, start = divmod((row - 1) * PIECE, NB) if row > 0 else (RT_DEV - 1, None)
    return pl.pallas_call(
        functools.partial(hash_kernel, row, tile, start),
        out_shape=jax.ShapeDtypeStruct((KB, PIECE), jnp.float32),
        in_specs=[SMEM, SMEM, VMEM, VMEM, ANY],
        out_specs=VMEM,
        scratch_shapes=[pltpu.VMEM((PIECE, LANES), jnp.float32)],
        cost_estimate=pl.CostEstimate(
            flops=PIECE * CT_DEV * NB * 2, bytes_accessed=PIECE * LANES * 4, transcendentals=0
        ),
        compiler_params=LIMIT,
        name=f"hash_{row}",
    )(seeds, meta, v, table, token)


def step_kernel(k, came, *refs):
    refs = list(refs)
    same, other = [refs.pop(0) for _ in range(2)] if k > 0 else [None] * 2
    inv, table = refs.pop(0), refs.pop(0)
    near = [refs.pop(0) for _ in range(4)] if k < NEAR else None
    far = [refs.pop(0) for _ in range(4)] if k < KB - 1 else None
    total_out = refs.pop(0) if k < KB - 1 else None
    table_out, spread_y, held, sem = refs
    col = lax.axis_index("pcol")
    me = lax.axis_index("prow")
    mine = col // 2 == k
    table_out[...] = table[...]

    @pl.when(mine)
    def _():
        if k < NEAR:
            fetch = pltpu.make_async_copy(near[1].at[:, k:], held, sem)
            fetch.start()
        s = jnp.sum(came[:, :1, :], axis=0)
        if k > 0:
            running = same[...] + other[...]
            s = s - running[k:k + 1, :]
        y = jnp.sum(inv[...].astype(jnp.float32) * s, axis=1, keepdims=True)
        if k < KB - 1:
            spread_y[...] = jnp.broadcast_to(y, (256, LANES)).reshape(GRID, 16, LANES)
            rows = [jnp.zeros((1, NB), jnp.float32)] * (k + 1)
            if k < NEAR:
                fetch.wait()
            for kk in range(k, KB - 1):
                part = jnp.zeros((16, NB), jnp.float32)
                for m in range(4):
                    for i in range(4):
                        if kk < NEAR:
                            tile = held[i, kk - k] if m == 1 else near[m][i, kk]
                            source = me ^ (4 * m + i)
                        else:
                            tile, source = far[m][i, kk - NEAR], me ^ (4 * i + m)
                        part = part + tile * jnp.concatenate([spread_y[source]] * GROUPS, axis=1)
                rows.append(jnp.sum(part, axis=0, keepdims=True))
            update = jnp.concatenate(rows, axis=0)
            if k > 0:
                update = update + jnp.where(col % 2 == 0, running, 0.0)
            total_out[...] = update
        eye = lax.broadcasted_iota(jnp.int32, (256, 256), 0) == lax.broadcasted_iota(jnp.int32, (256, 256), 1)
        table_out[KB - 1:KB, :] = jnp.sum(jnp.where(eye, y, 0.0), axis=0, keepdims=True)

    if k < KB - 1:
        @pl.when(jnp.logical_not(mine))
        def _():
            total_out[...] = jnp.zeros_like(total_out)


def step(k, came, running, inv, table, tiles):
    args = [came, *running, inv, table]
    shapes = [jax.ShapeDtypeStruct((KB, PIECE), jnp.float32)]
    in_specs = [VMEM] * len(args)
    if k < NEAR:
        args += tiles[:4]
        in_specs += [VMEM, ANY, VMEM, VMEM]
    if k < KB - 1:
        args += tiles[4:]
        in_specs += [VMEM] * 4
        shapes = [jax.ShapeDtypeStruct((KB, NB), jnp.float32)] + shapes
    return pl.pallas_call(
        functools.partial(step_kernel, k),
        out_shape=shapes,
        in_specs=in_specs,
        out_specs=[VMEM] * len(shapes),
        scratch_shapes=[
            pltpu.VMEM((GRID, 16, LANES), jnp.float32),
            pltpu.VMEM((4, max(NEAR - k, 1), 16, NB), jnp.float32),
            pltpu.SemaphoreType.DMA,
        ],
        compiler_params=LIMIT,
        name=f"step_{k}",
    )(*args)


def last_kernel(factor, owner, rhs, v, came, panel, table, out):
    row_index, col_index = lax.axis_index("prow"), lax.axis_index("pcol")
    my_tile = (row_index - owner[0] + GRID) & (GRID - 1)
    y = table[KB - 1:KB, :]
    residual = jnp.sum(came[:, :1, :], axis=0)
    theirs = came[(row_index + KB) & (GRID - 1), 1:, :]
    for at in range(0, ROWS, LANES):
        n = at // LANES
        part = panel[at:at + LANES, :].astype(jnp.float32) * y
        part = (part[:, :LANES] + part[:, LANES:]) * factor[at // NB]
        total = jnp.sum(part.T, axis=0, keepdims=True)
        given = jnp.where(col_index == 0, rhs[n:n + 1, :], 0.0)
        given = given - jnp.where(my_tile == col_index, v[n // GROUPS, n % GROUPS:n % GROUPS + 1, :], 0.0)
        if at < NB:
            shared = table[0:1, at:at + LANES] if at < PIECE else theirs[:, at - PIECE:at - PIECE + LANES]
            given = given - shared
            known = jnp.where(col_index == 2 * my_tile, residual[:, at:at + LANES], 0.0)
            given = jnp.where(my_tile < KB, known, given)
        else:
            piece, row = divmod(at - NB, PIECE)
            given = given - table[piece + 1:piece + 2, row:row + LANES]
        out[n:n + 1, :] = given - total


def last(factor, owner, rhs, v, came, panel, table):
    return pl.pallas_call(
        last_kernel,
        out_shape=jax.ShapeDtypeStruct((GRID, LANES), jnp.float32),
        in_specs=[SMEM] * 2 + [VMEM] * 5,
        out_specs=VMEM,
        compiler_params=LIMIT,
        name="last",
    )(factor, owner, rhs, v, came, panel, table)


def to_all(value, axis):
    return lax.all_to_all(jnp.broadcast_to(value[None], (GRID,) + value.shape), axis, 0, 0, tiled=True)


def exchange(value, mask):
    return lax.ppermute(value, "prow", [(i, i ^ mask) for i in range(GRID)])


def body(seeds, tile_owner, vector, rhs, panel, tile_scales, inverses):
    row_index = lax.axis_index("prow")
    col_index = lax.axis_index("pcol")
    anchor = tile_owner[0]
    block = col_index // 2
    first_tile = jnp.mod(row_index - anchor, GRID)
    my_tiles = jnp.arange(RT_DEV, dtype=jnp.int32) * GRID + first_tile
    scales = lax.dynamic_slice_in_dim(tile_scales, block, 1, 1)[:, 0]
    factor = jnp.where(my_tiles > block, scales, jnp.float32(0.0))

    scaled = (panel[:NB].astype(jnp.float32) * factor[0]).T.reshape(GRID, 16, NB)
    padded = jnp.pad(vector, (0, 2 * NB - vector.shape[0])).reshape(1, 2, NB)
    sent = jnp.concatenate([scaled, jnp.broadcast_to(padded, (GRID, 2, NB))], axis=1)
    came = lax.all_to_all(sent, "prow", 0, 0, tiled=True)

    edge = jnp.zeros((96,), jnp.float32)
    window = lax.dynamic_slice_in_dim(
        jnp.concatenate([edge, vector, edge]), 96 - 32 * jnp.mod(row_index, 4), WINDOW * LANES, 0
    ).reshape(WINDOW, LANES)
    parts = first_rows(
        tile_owner, seeds, window, rhs[:NB].reshape(1, NB), vector[:NB].reshape(1, NB)
    )

    early = first_tile < KB
    shared = jnp.where(early, jnp.mod(row_index + KB, GRID), row_index) * RT_DEV
    seed_rows = jnp.concatenate([
        lax.dynamic_slice_in_dim(seeds, row_index * RT_DEV + 1, RT_DEV - 1, 0),
        lax.dynamic_slice_in_dim(seeds, shared, 1, 0),
    ])
    meta = jnp.where(early, PIECE, 0).reshape(1)

    own = lax.dynamic_slice_in_dim(jnp.concatenate([came, came])[:, :16], anchor + 1, KB - 1, 0)
    v = came[:, 16:].reshape(GRID, 2 * NB)[:, :vector.shape[0]].reshape(CT_DEV, GROUPS, LANES)
    near, far, parts, v = lax.optimization_barrier((own[:NEAR], own[NEAR:], parts, v))
    near = jnp.stack([near] + [exchange(near, m) for m in (1, 2, 3)])
    far = jnp.stack([far] + [exchange(far, m) for m in (4, 8, 12)])
    table = hash_rows(seed_rows, meta, v, jnp.zeros((KB, PIECE), jnp.float32), parts, 0)
    part = jnp.sum(lax.all_to_all(parts, "pcol", 0, 0, tiled=True), axis=0)
    near, far, part, table = lax.optimization_barrier((near, far, part, table))
    first, second = exchange(far, 1), exchange(far, 2)
    across = [exchange(near, m) for m in (4, 8, 12)]
    far, first = lax.optimization_barrier((far, first))
    tiles = [near] + across + [far, first, second, exchange(far, 3)]
    came = to_all(jnp.concatenate([part, jnp.pad(table[:1], ((0, 0), (0, PIECE)))]), "prow")
    row = 1
    for _ in range(AHEAD):
        table = hash_rows(seed_rows, meta, v, table, part, row)
        row += 1

    running = ()
    for k in range(KB - 1):
        total, table = step(k, came, running, inverses, table, tiles)
        same = lax.ppermute(total, "pcol", [(2 * k + h, 2 * k + 2 + h) for h in range(2)])
        other = lax.ppermute(total, "pcol", [(2 * k + h, 2 * k + 3 - h) for h in range(2)])
        if k in GAPS:
            table = hash_rows(seed_rows, meta, v, table, total, row)
            row += 1
        running = (same, other)
    table = step(KB - 1, came, running, inverses, table, tiles)[0]

    sums = last(factor, tile_owner, rhs.reshape(GRID, LANES), v, came, panel, table)
    updated = jnp.sum(lax.all_to_all(sums, "pcol", 0, 0, tiled=True), axis=0)
    return (table[KB - 1], updated)


def solution(mesh):
    placed = (
        P(None, "pcol"),
        P(),
        P(("pcol", "prow")),
        P("prow"),
        P("prow", "pcol"),
        P("prow", None),
        P("pcol", None),
    )
    return jax.shard_map(
        body,
        mesh=mesh,
        in_specs=placed,
        out_specs=(P("pcol"), P(("prow", "pcol"))),
        check_vma=False,
    )
```

```python
import functools

import jax
import jax.numpy as jnp
from jax import lax
from jax.experimental import pallas as pl
from jax.experimental.pallas import tpu as pltpu
from jax.sharding import PartitionSpec as P

NB = 512
KB = 8
RT_DEV = 4
CT_DEV = 25
GRID = 16
ROWS = RT_DEV * NB
LANES = 128
GROUPS = NB // LANES
STRIP = 32
UNIT = 2.0 ** -40
NEAR = 4
PIECE = 256
WIDE = 64
WINDOW = 7
AHEAD = 2
GAPS = (1, 2, 3, 5)
BIAS = -127.5

VMEM = pl.BlockSpec(memory_space=pltpu.VMEM)
ANY = pl.BlockSpec(memory_space=pl.ANY)
SMEM = pl.BlockSpec(memory_space=pltpu.SMEM)
LIMIT = pltpu.CompilerParams(vmem_limit_bytes=6 * 1024 * 1024)


def shift_right(value, amount):
    return lax.shift_right_logical(value, jnp.full_like(value, amount))


def signed_hash(mixed):
    mixed = mixed ^ shift_right(mixed, 15)
    mixed = mixed * jnp.int32(747796405)
    mixed = mixed ^ shift_right(mixed, 13)
    mixed = mixed * jnp.int32(1274126177)
    return (mixed ^ jnp.int32(-2147483648)) ^ shift_right(mixed, 16)


def weighted(bases, seed, entries, sums):
    return [
        total + signed_hash(base + seed).astype(jnp.float32) * entry
        for base, entry, total in zip(bases, entries, sums)
    ]


def first_kernel(owner, seeds, window, rhs, vector, out, sums):
    row_index, col_index = lax.axis_index("prow"), lax.axis_index("pcol")
    anchor = owner[0]
    my_tile = (row_index - anchor + GRID) & (GRID - 1)
    group = (row_index * 25) >> 2
    bias = jnp.broadcast_to(jnp.sum(window[...], axis=0, keepdims=True) * jnp.float32(BIAS), (WIDE, LANES))
    u = lax.broadcasted_iota(jnp.int32, (WIDE, LANES), 1)
    t = lax.broadcasted_iota(jnp.int32, (WIDE, LANES), 0)

    def tile(k, carry):
        slot = ((anchor + k) & (GRID - 1)) * RT_DEV
        shifts = [
            seeds[slot, (group + i) >> 2] + (((group + i) & 3) * LANES) * jnp.int32(1103515245)
            for i in range(WINDOW)
        ]

        def strip(number, inner):
            base = ((number * WIDE + t) * NB + u) * jnp.int32(1103515245)
            totals = [bias, jnp.zeros((WIDE, LANES), jnp.float32)]
            for i in range(WINDOW):
                entries = jnp.broadcast_to(window[i:i + 1, :], (WIDE, LANES))
                totals[i % 2] = weighted([base], shifts[i], [entries], [totals[i % 2]])[0]
            sums[pl.ds(pl.multiple_of(number * WIDE, WIDE), WIDE), :] = totals[0] + totals[1]
            return inner

        lax.fori_loop(0, NB // WIDE, strip, 0)
        value = jnp.sum(sums[...].T, axis=0, keepdims=True) * jnp.float32(-UNIT)
        value = value + jnp.where((col_index == 0) & (k == my_tile), rhs[...], 0.0)
        value = value - jnp.where((row_index == 0) & (col_index == k), vector[...], 0.0)
        out[pl.ds(2 * k, 2), :, :] = jnp.broadcast_to(value[None], (2, 1, NB))
        return carry

    lax.fori_loop(0, KB, tile, 0)


def first_rows(tile_owner, seeds, window, rhs, vector):
    return pl.pallas_call(
        first_kernel,
        out_shape=jax.ShapeDtypeStruct((GRID, 1, NB), jnp.float32),
        in_specs=[SMEM, SMEM, VMEM, VMEM, VMEM],
        out_specs=VMEM,
        scratch_shapes=[pltpu.VMEM((NB, LANES), jnp.float32)],
        cost_estimate=pl.CostEstimate(flops=KB * NB * 1600, bytes_accessed=GRID * NB * 4, transcendentals=0),
        compiler_params=LIMIT,
        name="first_rows",
    )(tile_owner, seeds, window, rhs, vector)


def spread_kernel(owner, scales, vector, panel, out, held, sem):
    fetch = pltpu.make_async_copy(panel.at[pl.ds(0, NB)], held, sem)
    fetch.start()
    block = lax.axis_index("pcol") >> 1
    my_tile = (lax.axis_index("prow") - owner[0] + GRID) & (GRID - 1)
    factor = jnp.where(my_tile > block, scales[0, block], jnp.float32(0.0))
    length = vector.shape[1]
    out[:, 16:17, :] = jnp.broadcast_to(vector[:, :NB][None], (GRID, 1, NB))
    out[:, 17:18, :] = jnp.zeros((GRID, 1, NB), jnp.float32)
    out[:, 17:18, :length - NB] = jnp.broadcast_to(vector[:, NB:][None], (GRID, 1, length - NB))
    fetch.wait()
    out[:, :16, :] = (held[...].astype(jnp.float32) * factor).T.reshape(GRID, 16, NB)


def spread_parts(tile_owner, tile_scales, vector, panel):
    return pl.pallas_call(
        spread_kernel,
        out_shape=jax.ShapeDtypeStruct((GRID, 18, NB), jnp.float32),
        in_specs=[SMEM, SMEM, VMEM, ANY],
        out_specs=VMEM,
        scratch_shapes=[pltpu.VMEM((NB, 256), jnp.bfloat16), pltpu.SemaphoreType.DMA],
        compiler_params=LIMIT,
        name="spread_parts",
    )(tile_owner, tile_scales, vector, panel)


def hash_kernel(row, tile, start, seeds, meta, v, table, _, out, held):
    bias = jnp.sum(jnp.sum(v[...], axis=0), axis=0, keepdims=True) * jnp.float32(BIAS)
    begin = meta[0] if start is None else start

    def strip(number, carry):
        inner = begin + number * STRIP
        t = (inner + lax.broadcasted_iota(jnp.int32, (STRIP, LANES), 0)) * jnp.int32(NB)
        u = lax.broadcasted_iota(jnp.int32, (STRIP, LANES), 1)
        bases = [(t + u + jnp.int32(LANES * g)) * jnp.int32(1103515245) for g in range(GROUPS)]
        sums = [jnp.broadcast_to(bias, (STRIP, LANES))] + [jnp.zeros((STRIP, LANES), jnp.float32)] * (GROUPS - 1)
        for j in range(CT_DEV):
            entries = [jnp.broadcast_to(v[j, g:g + 1, :], (STRIP, LANES)) for g in range(GROUPS)]
            sums = weighted(bases, seeds[tile, j], entries, sums)
        total = (sums[0] + sums[1]) + (sums[2] + sums[3])
        held[pl.ds(pl.multiple_of(number * STRIP, STRIP), STRIP), :] = total
        return carry

    lax.fori_loop(0, PIECE // STRIP, strip, 0)
    out[...] = table[...]
    out[row + 1:row + 2, :] = jnp.sum(held[...].T, axis=0, keepdims=True) * jnp.float32(UNIT)


def hash_rows(seeds, meta, v, table, token, row):
    tile, start = divmod((row - 1) * PIECE, NB) if row > 0 else (RT_DEV - 1, None)
    return pl.pallas_call(
        functools.partial(hash_kernel, row, tile, start),
        out_shape=jax.ShapeDtypeStruct((KB, PIECE), jnp.float32),
        in_specs=[SMEM, SMEM, VMEM, VMEM, ANY],
        out_specs=VMEM,
        scratch_shapes=[pltpu.VMEM((PIECE, LANES), jnp.float32)],
        cost_estimate=pl.CostEstimate(
            flops=PIECE * CT_DEV * NB * 2, bytes_accessed=PIECE * LANES * 4, transcendentals=0
        ),
        compiler_params=LIMIT,
        name=f"hash_{row}",
    )(seeds, meta, v, table, token)


def step_kernel(k, came, *refs):
    refs = list(refs)
    same, other = [refs.pop(0) for _ in range(2)] if k > 0 else [None] * 2
    inv, table = refs.pop(0), refs.pop(0)
    near = [refs.pop(0) for _ in range(4)] if k < NEAR else None
    far = [refs.pop(0) for _ in range(4)] if k < KB - 1 else None
    total_out = refs.pop(0) if k < KB - 1 else None
    table_out, spread_y, held, sem = refs
    col = lax.axis_index("pcol")
    me = lax.axis_index("prow")
    mine = col // 2 == k
    table_out[...] = table[...]

    @pl.when(mine)
    def _():
        if k < NEAR:
            fetch = pltpu.make_async_copy(near[1].at[:, k:], held, sem)
            fetch.start()
        s = jnp.sum(came[:, :1, :], axis=0)
        if k > 0:
            running = same[...] + other[...]
            s = s - running[k:k + 1, :]
        y = jnp.sum(inv[...].astype(jnp.float32) * s, axis=1, keepdims=True)
        if k < KB - 1:
            spread_y[...] = jnp.broadcast_to(y, (256, LANES)).reshape(GRID, 16, LANES)
            rows = [jnp.zeros((1, NB), jnp.float32)] * (k + 1)
            if k < NEAR:
                fetch.wait()
            for kk in range(k, KB - 1):
                part = jnp.zeros((16, NB), jnp.float32)
                for m in range(4):
                    for i in range(4):
                        if kk < NEAR:
                            tile = held[i, kk - k] if m == 1 else near[m][i, kk]
                            source = me ^ (4 * m + i)
                        else:
                            tile, source = far[m][i, kk - NEAR], me ^ (4 * i + m)
                        part = part + tile * jnp.concatenate([spread_y[source]] * GROUPS, axis=1)
                rows.append(jnp.sum(part, axis=0, keepdims=True))
            update = jnp.concatenate(rows, axis=0)
            if k > 0:
                update = update + jnp.where(col % 2 == 0, running, 0.0)
            total_out[...] = update
        eye = lax.broadcasted_iota(jnp.int32, (256, 256), 0) == lax.broadcasted_iota(jnp.int32, (256, 256), 1)
        table_out[0:1, :] = jnp.sum(jnp.where(eye, y, 0.0), axis=0, keepdims=True)

    if k < KB - 1:
        @pl.when(jnp.logical_not(mine))
        def _():
            total_out[...] = jnp.zeros_like(total_out)


def step(k, came, running, inv, table, tiles):
    args = [came, *running, inv, table]
    shapes = [jax.ShapeDtypeStruct((KB, PIECE), jnp.float32)]
    in_specs = [VMEM] * len(args)
    if k < NEAR:
        args += tiles[:4]
        in_specs += [VMEM, ANY, VMEM, VMEM]
    if k < KB - 1:
        args += tiles[4:]
        in_specs += [VMEM] * 4
        shapes = [jax.ShapeDtypeStruct((KB, NB), jnp.float32)] + shapes
    return pl.pallas_call(
        functools.partial(step_kernel, k),
        out_shape=shapes,
        in_specs=in_specs,
        out_specs=[VMEM] * len(shapes),
        scratch_shapes=[
            pltpu.VMEM((GRID, 16, LANES), jnp.float32),
            pltpu.VMEM((4, max(NEAR - k, 1), 16, NB), jnp.float32),
            pltpu.SemaphoreType.DMA,
        ],
        compiler_params=LIMIT,
        name=f"step_{k}",
    )(*args)


def last_kernel(factor, owner, rhs, v, came, panel, table, out):
    row_index, col_index = lax.axis_index("prow"), lax.axis_index("pcol")
    my_tile = (row_index - owner[0] + GRID) & (GRID - 1)
    y = table[0:1, :]
    residual = jnp.sum(came[:, :1, :], axis=0)
    theirs = came[(row_index + KB) & (GRID - 1), 1:, :]
    for at in range(0, ROWS, LANES):
        n = at // LANES
        part = panel[at:at + LANES, :].astype(jnp.float32) * y
        part = (part[:, :LANES] + part[:, LANES:]) * factor[at // NB]
        total = jnp.sum(part.T, axis=0, keepdims=True)
        given = jnp.where(col_index == 0, rhs[n:n + 1, :], 0.0)
        given = given - jnp.where(my_tile == col_index, v[n // GROUPS, n % GROUPS:n % GROUPS + 1, :], 0.0)
        if at < NB:
            shared = table[1:2, at:at + LANES] if at < PIECE else theirs[:, at - PIECE:at - PIECE + LANES]
            given = given - shared
            known = jnp.where(col_index == 2 * my_tile, residual[:, at:at + LANES], 0.0)
            given = jnp.where(my_tile < KB, known, given)
        else:
            piece, row = divmod(at - NB, PIECE)
            given = given - table[piece + 2:piece + 3, row:row + LANES]
        out[n:n + 1, :] = given - total


def last(factor, owner, rhs, v, came, panel, table):
    return pl.pallas_call(
        last_kernel,
        out_shape=jax.ShapeDtypeStruct((GRID, LANES), jnp.float32),
        in_specs=[SMEM] * 2 + [VMEM] * 5,
        out_specs=VMEM,
        compiler_params=LIMIT,
        name="last",
    )(factor, owner, rhs, v, came, panel, table)


def to_all(value, axis):
    return lax.all_to_all(jnp.broadcast_to(value[None], (GRID,) + value.shape), axis, 0, 0, tiled=True)


def exchange(value, mask):
    return lax.ppermute(value, "prow", [(i, i ^ mask) for i in range(GRID)])


def body(seeds, tile_owner, vector, rhs, panel, tile_scales, inverses):
    row_index = lax.axis_index("prow")
    col_index = lax.axis_index("pcol")
    anchor = tile_owner[0]
    block = col_index // 2
    first_tile = jnp.mod(row_index - anchor, GRID)
    my_tiles = jnp.arange(RT_DEV, dtype=jnp.int32) * GRID + first_tile
    scales = lax.dynamic_slice_in_dim(tile_scales, block, 1, 1)[:, 0]
    factor = jnp.where(my_tiles > block, scales, jnp.float32(0.0))

    sent = spread_parts(tile_owner, tile_scales, vector.reshape(1, -1), panel)
    came = lax.all_to_all(sent, "prow", 0, 0, tiled=True)

    edge = jnp.zeros((96,), jnp.float32)
    window = lax.dynamic_slice_in_dim(
        jnp.concatenate([edge, vector, edge]), 96 - 32 * jnp.mod(row_index, 4), WINDOW * LANES, 0
    ).reshape(WINDOW, LANES)
    parts = first_rows(
        tile_owner, seeds, window, rhs[:NB].reshape(1, NB), vector[:NB].reshape(1, NB)
    )

    early = first_tile < KB
    shared = jnp.where(early, jnp.mod(row_index + KB, GRID), row_index) * RT_DEV
    seed_rows = jnp.concatenate([
        lax.dynamic_slice_in_dim(seeds, row_index * RT_DEV + 1, RT_DEV - 1, 0),
        lax.dynamic_slice_in_dim(seeds, shared, 1, 0),
    ])
    meta = jnp.where(early, PIECE, 0).reshape(1)

    own = lax.dynamic_slice_in_dim(jnp.concatenate([came, came])[:, :16], anchor + 1, KB - 1, 0)
    v = came[:, 16:].reshape(GRID, 2 * NB)[:, :vector.shape[0]].reshape(CT_DEV, GROUPS, LANES)
    near, far, parts, v = lax.optimization_barrier((own[:NEAR], own[NEAR:], parts, v))
    near = jnp.stack([near] + [exchange(near, m) for m in (1, 2, 3)])
    far = jnp.stack([far] + [exchange(far, m) for m in (4, 8, 12)])
    table = hash_rows(seed_rows, meta, v, jnp.zeros((KB, PIECE), jnp.float32), parts, 0)
    part = jnp.sum(lax.all_to_all(parts, "pcol", 0, 0, tiled=True), axis=0)
    near, far, part, table = lax.optimization_barrier((near, far, part, table))
    first, second = exchange(far, 1), exchange(far, 2)
    across = [exchange(near, m) for m in (4, 8, 12)]
    far, first = lax.optimization_barrier((far, first))
    tiles = [near] + across + [far, first, second, exchange(far, 3)]
    came = to_all(jnp.concatenate([part, jnp.pad(table[1:2], ((0, 0), (0, PIECE)))]), "prow")
    row = 1
    for _ in range(AHEAD):
        table = hash_rows(seed_rows, meta, v, table, part, row)
        row += 1

    running = ()
    for k in range(KB - 1):
        total, table = step(k, came, running, inverses, table, tiles)
        same = lax.ppermute(total, "pcol", [(2 * k + h, 2 * k + 2 + h) for h in range(2)])
        other = lax.ppermute(total, "pcol", [(2 * k + h, 2 * k + 3 - h) for h in range(2)])
        if k in GAPS:
            table = hash_rows(seed_rows, meta, v, table, total, row)
            row += 1
        running = (same, other)
    table = step(KB - 1, came, running, inverses, table, tiles)[0]

    sums = last(factor, tile_owner, rhs.reshape(GRID, LANES), v, came, panel, table)
    updated = jnp.sum(lax.all_to_all(sums, "pcol", 0, 0, tiled=True), axis=0)
    return (table[0], updated)


def solution(mesh):
    placed = (
        P(None, "pcol"),
        P(),
        P(("pcol", "prow")),
        P("prow"),
        P("prow", "pcol"),
        P("prow", None),
        P("pcol", None),
    )
    return jax.shard_map(
        body,
        mesh=mesh,
        in_specs=placed,
        out_specs=(P("pcol"), P(("prow", "pcol"))),
        check_vma=False,
    )
```

```python
import functools

import jax
import jax.numpy as jnp
from jax import lax
from jax.experimental import pallas as pl
from jax.experimental.pallas import tpu as pltpu
from jax.sharding import PartitionSpec as P

NB = 512
KB = 8
RT_DEV = 4
CT_DEV = 25
GRID = 16
ROWS = RT_DEV * NB
LANES = 128
GROUPS = NB // LANES
STRIP = 32
UNIT = 2.0 ** -40
NEAR = 4
PIECE = 256
WIDE = 64
WINDOW = 7
AHEAD = 2
GAPS = (1, 2, 4)
BIAS = -127.5

VMEM = pl.BlockSpec(memory_space=pltpu.VMEM)
ANY = pl.BlockSpec(memory_space=pl.ANY)
SMEM = pl.BlockSpec(memory_space=pltpu.SMEM)
LIMIT = pltpu.CompilerParams(vmem_limit_bytes=6 * 1024 * 1024)


def shift_right(value, amount):
    return lax.shift_right_logical(value, jnp.full_like(value, amount))


def signed_hash(mixed):
    mixed = mixed ^ shift_right(mixed, 15)
    mixed = mixed * jnp.int32(747796405)
    mixed = mixed ^ shift_right(mixed, 13)
    mixed = mixed * jnp.int32(1274126177)
    return (mixed ^ jnp.int32(-2147483648)) ^ shift_right(mixed, 16)


def weighted(bases, seed, entries, sums):
    return [
        total + signed_hash(base + seed).astype(jnp.float32) * entry
        for base, entry, total in zip(bases, entries, sums)
    ]


def first_kernel(owner, seeds, window, rhs, vector, out, sums):
    row_index, col_index = lax.axis_index("prow"), lax.axis_index("pcol")
    anchor = owner[0]
    my_tile = (row_index - anchor + GRID) & (GRID - 1)
    group = (row_index * 25) >> 2
    bias = jnp.broadcast_to(jnp.sum(window[...], axis=0, keepdims=True) * jnp.float32(BIAS), (WIDE, LANES))
    u = lax.broadcasted_iota(jnp.int32, (WIDE, LANES), 1)
    t = lax.broadcasted_iota(jnp.int32, (WIDE, LANES), 0)

    def tile(k, carry):
        slot = ((anchor + k) & (GRID - 1)) * RT_DEV
        shifts = [
            seeds[slot, (group + i) >> 2] + (((group + i) & 3) * LANES) * jnp.int32(1103515245)
            for i in range(WINDOW)
        ]

        def strip(number, inner):
            base = ((number * WIDE + t) * NB + u) * jnp.int32(1103515245)
            totals = [bias, jnp.zeros((WIDE, LANES), jnp.float32)]
            for i in range(WINDOW):
                entries = jnp.broadcast_to(window[i:i + 1, :], (WIDE, LANES))
                totals[i % 2] = weighted([base], shifts[i], [entries], [totals[i % 2]])[0]
            sums[pl.ds(pl.multiple_of(number * WIDE, WIDE), WIDE), :] = totals[0] + totals[1]
            return inner

        lax.fori_loop(0, NB // WIDE, strip, 0)
        value = jnp.sum(sums[...].T, axis=0, keepdims=True) * jnp.float32(-UNIT)
        value = value + jnp.where((col_index == 0) & (k == my_tile), rhs[...], 0.0)
        value = value - jnp.where((row_index == 0) & (col_index == k), vector[...], 0.0)
        out[pl.ds(2 * k, 2), :, :] = jnp.broadcast_to(value[None], (2, 1, NB))
        return carry

    lax.fori_loop(0, KB, tile, 0)


def first_rows(tile_owner, seeds, window, rhs, vector):
    return pl.pallas_call(
        first_kernel,
        out_shape=jax.ShapeDtypeStruct((GRID, 1, NB), jnp.float32),
        in_specs=[SMEM, SMEM, VMEM, VMEM, VMEM],
        out_specs=VMEM,
        scratch_shapes=[pltpu.VMEM((NB, LANES), jnp.float32)],
        cost_estimate=pl.CostEstimate(flops=KB * NB * 1600, bytes_accessed=GRID * NB * 4, transcendentals=0),
        compiler_params=LIMIT,
        name="first_rows",
    )(tile_owner, seeds, window, rhs, vector)


def spread_kernel(owner, scales, vector, panel, out, held, sem):
    fetch = pltpu.make_async_copy(panel.at[pl.ds(0, NB)], held, sem)
    fetch.start()
    block = lax.axis_index("pcol") >> 1
    my_tile = (lax.axis_index("prow") - owner[0] + GRID) & (GRID - 1)
    factor = jnp.where(my_tile > block, scales[0, block], jnp.float32(0.0))
    length = vector.shape[1]
    out[:, 16:17, :] = jnp.broadcast_to(vector[:, :NB][None], (GRID, 1, NB))
    out[:, 17:18, :] = jnp.zeros((GRID, 1, NB), jnp.float32)
    out[:, 17:18, :length - NB] = jnp.broadcast_to(vector[:, NB:][None], (GRID, 1, length - NB))
    fetch.wait()
    out[:, :16, :] = (held[...].astype(jnp.float32) * factor).T.reshape(GRID, 16, NB)


def spread_parts(tile_owner, tile_scales, vector, panel):
    return pl.pallas_call(
        spread_kernel,
        out_shape=jax.ShapeDtypeStruct((GRID, 18, NB), jnp.float32),
        in_specs=[SMEM, SMEM, VMEM, ANY],
        out_specs=VMEM,
        scratch_shapes=[pltpu.VMEM((NB, 256), jnp.bfloat16), pltpu.SemaphoreType.DMA],
        compiler_params=LIMIT,
        name="spread_parts",
    )(tile_owner, tile_scales, vector, panel)


def hash_kernel(row, tile, start, seeds, meta, v, table, _, out, held):
    bias = jnp.sum(jnp.sum(v[...], axis=0), axis=0, keepdims=True) * jnp.float32(BIAS)
    begin = meta[0] if start is None else start

    def strip(number, carry):
        inner = begin + number * STRIP
        t = (inner + lax.broadcasted_iota(jnp.int32, (STRIP, LANES), 0)) * jnp.int32(NB)
        u = lax.broadcasted_iota(jnp.int32, (STRIP, LANES), 1)
        bases = [(t + u + jnp.int32(LANES * g)) * jnp.int32(1103515245) for g in range(GROUPS)]
        sums = [jnp.broadcast_to(bias, (STRIP, LANES))] + [jnp.zeros((STRIP, LANES), jnp.float32)] * (GROUPS - 1)
        for j in range(CT_DEV):
            entries = [jnp.broadcast_to(v[j, g:g + 1, :], (STRIP, LANES)) for g in range(GROUPS)]
            sums = weighted(bases, seeds[tile, j], entries, sums)
        total = (sums[0] + sums[1]) + (sums[2] + sums[3])
        held[pl.ds(pl.multiple_of(number * STRIP, STRIP), STRIP), :] = total
        return carry

    lax.fori_loop(0, PIECE // STRIP, strip, 0)
    out[...] = table[...]
    out[row + 1:row + 2, :] = jnp.sum(held[...].T, axis=0, keepdims=True) * jnp.float32(UNIT)


def hash_rows(seeds, meta, v, table, token, row):
    tile, start = divmod((row - 1) * PIECE, NB) if row > 0 else (RT_DEV - 1, None)
    return pl.pallas_call(
        functools.partial(hash_kernel, row, tile, start),
        out_shape=jax.ShapeDtypeStruct((KB, PIECE), jnp.float32),
        in_specs=[SMEM, SMEM, VMEM, VMEM, ANY],
        out_specs=VMEM,
        scratch_shapes=[pltpu.VMEM((PIECE, LANES), jnp.float32)],
        cost_estimate=pl.CostEstimate(
            flops=PIECE * CT_DEV * NB * 2, bytes_accessed=PIECE * LANES * 4, transcendentals=0
        ),
        compiler_params=LIMIT,
        name=f"hash_{row}",
    )(seeds, meta, v, table, token)


def step_kernel(k, came, *refs):
    refs = list(refs)
    same, other = [refs.pop(0) for _ in range(2)] if k > 0 else [None] * 2
    inv, table = refs.pop(0), refs.pop(0)
    near = [refs.pop(0) for _ in range(4)] if k < NEAR else None
    far = [refs.pop(0) for _ in range(4)] if k < KB - 1 else None
    total_out = refs.pop(0) if k < KB - 1 else None
    table_out, spread_y, held, sem = refs
    col = lax.axis_index("pcol")
    me = lax.axis_index("prow")
    mine = col // 2 == k
    table_out[...] = table[...]

    @pl.when(mine)
    def _():
        if k < NEAR:
            fetch = pltpu.make_async_copy(near[1].at[:, k:], held, sem)
            fetch.start()
        s = jnp.sum(came[:, :1, :], axis=0)
        if k > 0:
            running = same[...] + other[...]
            s = s - running[k:k + 1, :]
        y = jnp.sum(inv[...].astype(jnp.float32) * s, axis=1, keepdims=True)
        if k < KB - 1:
            spread_y[...] = jnp.broadcast_to(y, (256, LANES)).reshape(GRID, 16, LANES)
            rows = [jnp.zeros((1, NB), jnp.float32)] * (k + 1)
            if k < NEAR:
                fetch.wait()
            for kk in range(k, KB - 1):
                part = jnp.zeros((16, NB), jnp.float32)
                for m in range(4):
                    for i in range(4):
                        if kk < NEAR:
                            tile = held[i, kk - k] if m == 1 else near[m][i, kk]
                            source = me ^ (4 * m + i)
                        else:
                            tile, source = far[m][i, kk - NEAR], me ^ (4 * i + m)
                        part = part + tile * jnp.concatenate([spread_y[source]] * GROUPS, axis=1)
                rows.append(jnp.sum(part, axis=0, keepdims=True))
            update = jnp.concatenate(rows, axis=0)
            if k > 0:
                update = update + jnp.where(col % 2 == 0, running, 0.0)
            total_out[...] = update
        eye = lax.broadcasted_iota(jnp.int32, (256, 256), 0) == lax.broadcasted_iota(jnp.int32, (256, 256), 1)
        table_out[0:1, :] = jnp.sum(jnp.where(eye, y, 0.0), axis=0, keepdims=True)

    if k < KB - 1:
        @pl.when(jnp.logical_not(mine))
        def _():
            total_out[...] = jnp.zeros_like(total_out)


def step(k, came, running, inv, table, tiles):
    args = [came, *running, inv, table]
    shapes = [jax.ShapeDtypeStruct((KB, PIECE), jnp.float32)]
    in_specs = [VMEM] * len(args)
    if k < NEAR:
        args += tiles[:4]
        in_specs += [VMEM, ANY, VMEM, VMEM]
    if k < KB - 1:
        args += tiles[4:]
        in_specs += [VMEM] * 4
        shapes = [jax.ShapeDtypeStruct((KB, NB), jnp.float32)] + shapes
    return pl.pallas_call(
        functools.partial(step_kernel, k),
        out_shape=shapes,
        in_specs=in_specs,
        out_specs=[VMEM] * len(shapes),
        scratch_shapes=[
            pltpu.VMEM((GRID, 16, LANES), jnp.float32),
            pltpu.VMEM((4, max(NEAR - k, 1), 16, NB), jnp.float32),
            pltpu.SemaphoreType.DMA,
        ],
        compiler_params=LIMIT,
        name=f"step_{k}",
    )(*args)


def last_kernel(factor, owner, rhs, v, came, panel, table, out):
    row_index, col_index = lax.axis_index("prow"), lax.axis_index("pcol")
    my_tile = (row_index - owner[0] + GRID) & (GRID - 1)
    y = table[0:1, :]
    residual = jnp.sum(came[:, :1, :], axis=0)
    theirs = came[(row_index + KB) & (GRID - 1), 1:, :]
    for at in range(0, ROWS, LANES):
        n = at // LANES
        part = panel[at:at + LANES, :].astype(jnp.float32) * y
        part = (part[:, :LANES] + part[:, LANES:]) * factor[at // NB]
        total = jnp.sum(part.T, axis=0, keepdims=True)
        given = jnp.where(col_index == 0, rhs[n:n + 1, :], 0.0)
        given = given - jnp.where(my_tile == col_index, v[n // GROUPS, n % GROUPS:n % GROUPS + 1, :], 0.0)
        if at < NB:
            shared = table[1:2, at:at + LANES] if at < PIECE else theirs[:, at - PIECE:at - PIECE + LANES]
            given = given - shared
            known = jnp.where(col_index == 2 * my_tile, residual[:, at:at + LANES], 0.0)
            given = jnp.where(my_tile < KB, known, given)
        else:
            piece, row = divmod(at - NB, PIECE)
            given = given - table[piece + 2:piece + 3, row:row + LANES]
        out[n:n + 1, :] = given - total


def last(factor, owner, rhs, v, came, panel, table):
    return pl.pallas_call(
        last_kernel,
        out_shape=jax.ShapeDtypeStruct((GRID, LANES), jnp.float32),
        in_specs=[SMEM] * 2 + [VMEM] * 5,
        out_specs=VMEM,
        compiler_params=LIMIT,
        name="last",
    )(factor, owner, rhs, v, came, panel, table)


def to_all(value, axis):
    return lax.all_to_all(jnp.broadcast_to(value[None], (GRID,) + value.shape), axis, 0, 0, tiled=True)


def exchange(value, mask):
    return lax.ppermute(value, "prow", [(i, i ^ mask) for i in range(GRID)])


def body(seeds, tile_owner, vector, rhs, panel, tile_scales, inverses):
    row_index = lax.axis_index("prow")
    col_index = lax.axis_index("pcol")
    anchor = tile_owner[0]
    block = col_index // 2
    first_tile = jnp.mod(row_index - anchor, GRID)
    my_tiles = jnp.arange(RT_DEV, dtype=jnp.int32) * GRID + first_tile
    scales = lax.dynamic_slice_in_dim(tile_scales, block, 1, 1)[:, 0]
    factor = jnp.where(my_tiles > block, scales, jnp.float32(0.0))

    sent = spread_parts(tile_owner, tile_scales, vector.reshape(1, -1), panel)
    came = lax.all_to_all(sent, "prow", 0, 0, tiled=True)

    edge = jnp.zeros((96,), jnp.float32)
    window = lax.dynamic_slice_in_dim(
        jnp.concatenate([edge, vector, edge]), 96 - 32 * jnp.mod(row_index, 4), WINDOW * LANES, 0
    ).reshape(WINDOW, LANES)
    parts = first_rows(
        tile_owner, seeds, window, rhs[:NB].reshape(1, NB), vector[:NB].reshape(1, NB)
    )

    early = first_tile < KB
    shared = jnp.where(early, jnp.mod(row_index + KB, GRID), row_index) * RT_DEV
    seed_rows = jnp.concatenate([
        lax.dynamic_slice_in_dim(seeds, row_index * RT_DEV + 1, RT_DEV - 1, 0),
        lax.dynamic_slice_in_dim(seeds, shared, 1, 0),
    ])
    meta = jnp.where(early, PIECE, 0).reshape(1)

    own = lax.dynamic_slice_in_dim(jnp.concatenate([came, came])[:, :16], anchor + 1, KB - 1, 0)
    v = came[:, 16:].reshape(GRID, 2 * NB)[:, :vector.shape[0]].reshape(CT_DEV, GROUPS, LANES)
    near, far, parts, v = lax.optimization_barrier((own[:NEAR], own[NEAR:], parts, v))
    near = jnp.stack([near] + [exchange(near, m) for m in (1, 2, 3)])
    far = jnp.stack([far] + [exchange(far, m) for m in (4, 8, 12)])
    table = hash_rows(seed_rows, meta, v, jnp.zeros((KB, PIECE), jnp.float32), parts, 0)
    part = jnp.sum(lax.all_to_all(parts, "pcol", 0, 0, tiled=True), axis=0)
    near, far, part, table = lax.optimization_barrier((near, far, part, table))
    shared_sum = table[1:2]
    first, second = exchange(far, 1), exchange(far, 2)
    across = [exchange(near, m) for m in (4, 8, 12)]
    table = hash_rows(seed_rows, meta, v, table, part, 1)
    far, first, table = lax.optimization_barrier((far, first, table))
    tiles = [near] + across + [far, first, second, exchange(far, 3)]
    came = to_all(jnp.concatenate([part, jnp.pad(shared_sum, ((0, 0), (0, PIECE)))]), "prow")
    row = 2
    for _ in range(AHEAD):
        table = hash_rows(seed_rows, meta, v, table, part, row)
        row += 1

    running = ()
    for k in range(KB - 1):
        total, table = step(k, came, running, inverses, table, tiles)
        same = lax.ppermute(total, "pcol", [(2 * k + h, 2 * k + 2 + h) for h in range(2)])
        other = lax.ppermute(total, "pcol", [(2 * k + h, 2 * k + 3 - h) for h in range(2)])
        if k in GAPS:
            table = hash_rows(seed_rows, meta, v, table, total, row)
            row += 1
        running = (same, other)
    table = step(KB - 1, came, running, inverses, table, tiles)[0]

    sums = last(factor, tile_owner, rhs.reshape(GRID, LANES), v, came, panel, table)
    updated = jnp.sum(lax.all_to_all(sums, "pcol", 0, 0, tiled=True), axis=0)
    return (table[0], updated)


def solution(mesh):
    placed = (
        P(None, "pcol"),
        P(),
        P(("pcol", "prow")),
        P("prow"),
        P("prow", "pcol"),
        P("prow", None),
        P("pcol", None),
    )
    return jax.shard_map(
        body,
        mesh=mesh,
        in_specs=placed,
        out_specs=(P("pcol"), P(("prow", "pcol"))),
        check_vma=False,
    )
```
